32 devices in a mesh: slab: 2 (over core), corpus: 16 (over z, y, x).
Axes of the slice: x: 2, y: 2, z: 4, core: 2. Of those that a mesh axis runs over, the one named last changes fastest.
Arguments:
- vectors: bfloat16 [65536, 128], P(('slab', 'corpus')), parts along dimension 0, may hold values from -1.796875 to 1.796875
- docs: int32 [65536], P(('slab', 'corpus')), parts along dimension 0, may hold values from 0 to 63
- prior: float32 [65536], P(('slab', 'corpus')), parts along dimension 0, may hold values from 0.5 to 3
Outputs:
- best: float32 [65536], P(('slab', 'corpus')), parts along dimension 0
The draws below stay inside these ranges and needn't reach their ends.
There are 2 independent parts, one for each index of `slab`. The reference program is written for one: setup_inputs(seed, part) draws one part's arguments, and reference() takes and returns one part's arrays. A program takes and returns all parts, laid end to end along the dimension named above; each array names one. Nothing has to cross between parts.
All inputs are finite; a program needn't handle non-finite values.
Results may differ from the reference program's by a relative error of at most 0.0003.
Values may be sent and summed in bfloat16 or wider, within the bound.
No kernel may reach another device: no remote copies, remote signals or barrier semaphores. Data moves between devices by JAX's collectives and lax.ppermute only.
A program may use at most 128 MiB of HBM per device.

```python
import jax
import jax.numpy as jnp
from jax import lax

DIM = 128
TOK_DEV = 2048
ROUNDS = 4
DOCS = 64
TOKENS = 32768
N_CORPUS = 16


def touch_ends(values, key, least, largest):
    shape = values.shape
    spot = [jax.random.randint(jax.random.fold_in(key, axis), (), 0, shape[axis]) for axis in range(len(shape))]
    values = values.at[tuple(spot)].set(least)
    longest = shape.index(max(shape))
    spot[longest] = (spot[longest] + 1) % shape[longest]
    return values.at[tuple(spot)].set(largest)


def block_levels(own_key, dims, pieces, least, high):
    gain, own = 1.0, jax.random.fold_in(own_key, 6)
    for position, blocks in pieces:
        draws = jnp.exp(jax.random.uniform(jax.random.fold_in(own, position), (blocks,), jnp.float32, least / len(pieces), high / len(pieces)))
        gain = gain * jnp.repeat(draws, dims[position] // blocks).reshape([-1 if axis == position else 1 for axis in range(len(dims))])
    return gain


def scatter_about(own_key, dims, spread, reach, pieces=(), kind=jnp.bfloat16):
    loudness = block_levels(own_key, dims, pieces, -0.22, 0.18) if pieces else 1.0
    values = jax.random.normal(own_key, dims, jnp.float32) * spread * loudness
    return jnp.minimum(jnp.maximum(values, -reach), reach).astype(kind)


def setup_inputs(seed: int = 0, part: int = 0) -> dict:
    key_of = jax.random.split(jax.random.key(seed), 4)
    part_splits = jax.random.split(jax.random.fold_in(key_of[3], part), 4)
    return {
        "vectors": scatter_about(part_splits[0], (TOKENS, DIM), (DIM ** -0.25), 1.796875, ((0, 16),)),
        "docs": touch_ends(jax.random.randint(part_splits[1], (TOKENS,), 0, DOCS), jax.random.fold_in(part_splits[1], 1), 0, DOCS - 1).astype(jnp.int32),
        "prior": jnp.clip(0.5 + 2.5 * jax.random.uniform(part_splits[2], (TOKENS,), jnp.float32) ** block_levels(part_splits[2], (TOKENS,), ((0, 16),), -0.2, 0.2), 0.5, 3.0),
    }


NEG = -1e30


def one_tile(args):
    left, left_tags, right, right_tags = args
    scores = jnp.dot(left, right.T, precision=lax.Precision.HIGHEST)
    scores = jnp.where(left_tags[:, None] == right_tags[None, :], NEG, scores)
    return jnp.max(scores, axis=1), jnp.max(scores, axis=0)


def reference(vectors, docs, prior):
    blocks = vectors.astype(jnp.float32).reshape(N_CORPUS, TOK_DEV, DIM)
    labels = docs.reshape(N_CORPUS, TOK_DEV)
    best = prior.reshape(N_CORPUS, TOK_DEV)
    for dist in range(1, ROUNDS + 1):
        others = jnp.roll(blocks, dist, axis=0)
        other_labels = jnp.roll(labels, dist, axis=0)
        rowmax, colmax = lax.map(one_tile, (blocks, labels, others, other_labels))
        best = jnp.maximum(best, rowmax)
        best = jnp.maximum(best, jnp.roll(colmax, -dist, axis=0))
    return best.reshape(TOKENS)
```

```python
import functools

import jax
import jax.numpy as jnp
from jax import lax
from jax.experimental import pallas as pl
from jax.experimental.pallas import tpu as pltpu
from jax.sharding import PartitionSpec as P

ROUNDS = 4
NEG = -1e30
MARK = 2.0**50
LANES = 128
ROWS = 256
VMEM = 48 * 2**20


def routes(slabs, count):
    layer, ring, pair = [], [], []
    for slab in range(slabs):
        for block in range(count):
            place = block % ROUNDS

            def device(position):
                position = position % count
                return slab * count + (count - 1 - position if slab % 2 else position)

            layer.append((device(block), device(block - ROUNDS if place == 0 else block + ROUNDS)))
            ring.append((device(block), device(block - place + (place + 1) % ROUNDS)))
            if place < 2:
                pair.append((device(block), device(block + 2)))
    return layer, ring, pair


def backwards(pairs):
    return [(target, source) for source, target in pairs]


def pack_kernel(vec_ref, tag_ref, *outs):
    rows = vec_ref.shape[0] // len(outs)
    for index, out in enumerate(outs):
        out[:rows] = vec_ref[index * rows : (index + 1) * rows]
        out[rows:] = tag_ref[...]


def pack(vectors, tags, parts):
    count, dim = vectors.shape
    shape = jax.ShapeDtypeStruct((count // parts + tags.shape[0], dim), vectors.dtype)
    return pl.pallas_call(
        pack_kernel,
        out_shape=[shape] * parts,
        compiler_params=pltpu.CompilerParams(vmem_limit_bytes=VMEM),
        name="pack",
    )(vectors, tags)


def mark(tags, out, value):
    lane = lax.broadcasted_iota(jnp.int32, (LANES, LANES), 0).astype(jnp.float32)
    for row in range(tags.shape[0]):
        hit = jnp.where(tags[row : row + 1].astype(jnp.float32) == lane, jnp.float32(value), jnp.float32(0.0))
        out[row * LANES : (row + 1) * LANES] = hit.T.astype(jnp.bfloat16)


def tile(left, left_marks, right, right_marks, rowacc, col, fresh_row, fresh_col):
    wide = jnp.concatenate([right, right_marks], axis=1)
    columns = wide.shape[0]
    colmax = None
    for start in range(0, left.shape[0], ROWS):
        here = slice(start, start + ROWS)
        tall = jnp.concatenate([left[here], left_marks[here]], axis=1)
        scores = lax.dot_general(tall, wide, (((1,), (1,)), ((), ())), preferred_element_type=jnp.float32)
        best = scores[:, :LANES]
        for lane in range(LANES, columns, LANES):
            best = jnp.maximum(best, scores[:, lane : lane + LANES])
        rowacc[here] = best if fresh_row else jnp.maximum(rowacc[here], best)
        over = jnp.max(scores.reshape(ROWS // 8, 8, columns), axis=0)
        colmax = over if colmax is None else jnp.maximum(colmax, over)
    colmax = jnp.max(colmax, axis=0, keepdims=True)
    col[...] = colmax if fresh_col else jnp.maximum(col[...], colmax)


def fold(rowacc):
    return jnp.max(rowacc[...].reshape(rowacc.shape[0] // LANES, LANES, LANES), axis=2)


def first_kernel(has_pair, own, own_tags, z1, p1, q1, own_row, own_col, z_row, p_col, q_col,
                 own_m, z_m, p_m, q_m, own_acc, z_acc):
    half = own.shape[0] // 2
    mark(own_tags[...], own_m, -MARK)
    mark(z1[half:], z_m, MARK)
    mark(p1[half:], p_m, MARK)
    tile(own[...], own_m[...], p1[:half], p_m[:half], own_acc, p_col, True, True)
    tile(z1[:half], -z_m[:half], p1[:half], p_m[:half], z_acc, p_col, True, False)
    tile(z1[:half], z_m[:half], own[...], own_m[...], z_acc, own_col, False, True)
    q_col[...] = jnp.full(q_col.shape, NEG, jnp.float32)

    @pl.when(has_pair[0] > 0)
    def _():
        mark(q1[half:], q_m, MARK)
        tile(own[...], own_m[...], q1[:half], q_m[:half], own_acc, q_col, False, False)
        tile(z1[:half], -z_m[:half], q1[:half], q_m[:half], z_acc, q_col, False, False)

    own_row[...] = fold(own_acc)
    z_row[...] = fold(z_acc)


def second_kernel(has_pair, own, own_tags, z1, p1, q1, z2, p2, q2, own_row1, own_col1, z_row1, p_col1, q_col1,
                  own_out, z_out, p_out, q_out, own_m, z_m, p_m, q_m, own_acc, z_acc, own_col, p_col, q_col):
    half = own.shape[0] // 2
    mark(own_tags[...], own_m, -MARK)
    mark(z1[half:], z_m, MARK)
    mark(p1[half:], p_m, MARK)
    p_a, p_b = p_col.at[:, :half], p_col.at[:, half:]
    q_a, q_b = q_col.at[:, :half], q_col.at[:, half:]
    z_a, z_b = z_acc.at[:half], z_acc.at[half:]
    p_a[...] = p_col1[...]
    q_a[...] = q_col1[...]
    q_b[...] = jnp.full(q_b.shape, NEG, jnp.float32)
    own_col[...] = own_col1[...]
    tile(own[...], own_m[...], p2[:half], p_m[half:], own_acc, p_b, True, True)
    tile(z1[:half], -z_m[:half], p2[:half], p_m[half:], z_a, p_b, True, False)
    tile(z2[:half], -z_m[half:], p2[:half], p_m[half:], z_b, p_b, True, False)
    tile(z2[:half], -z_m[half:], p1[:half], p_m[:half], z_b, p_a, False, False)
    tile(z2[:half], z_m[half:], own[...], own_m[...], z_b, own_col, False, False)

    @pl.when(has_pair[0] > 0)
    def _():
        mark(q1[half:], q_m, MARK)
        tile(own[...], own_m[...], q2[:half], q_m[half:], own_acc, q_b, False, False)
        tile(z1[:half], -z_m[:half], q2[:half], q_m[half:], z_a, q_b, False, False)
        tile(z2[:half], -z_m[half:], q2[:half], q_m[half:], z_b, q_b, False, False)
        tile(z2[:half], -z_m[half:], q1[:half], q_m[:half], z_b, q_a, False, False)

    own_out[...] = jnp.maximum(jnp.maximum(own_row1[...], fold(own_acc)), own_col[...].reshape(own_out.shape))
    z_row = fold(z_acc)
    rows = z_row.shape[0] // 2
    z_out[:rows] = jnp.maximum(z_row1[...], z_row[:rows])
    z_out[rows:] = z_row[rows:]
    p_out[...] = p_col[...].reshape(p_out.shape)
    q_out[...] = q_col[...].reshape(q_out.shape)


def per_device(slabs, count, vectors, docs, prior):
    axes = ("slab", "corpus")
    tokens = vectors.shape[0]
    half = tokens // 2
    f32 = jnp.float32
    layer, ring, pair = routes(slabs, count)
    block = lax.axis_index("corpus")
    block = jnp.where(lax.axis_index("slab") % 2 == 1, count - 1 - block, block)
    has_pair = (block % ROUNDS >= 2).astype(jnp.int32).reshape(1)
    tags = docs.reshape(tokens // LANES, LANES).astype(jnp.bfloat16)
    halves = pack(vectors, tags, 2)
    (z1, p1, q1), (z2, p2, q2) = [
        [lax.ppermute(part, axes, pairs) for pairs in (layer, ring, pair)] for part in halves
    ]
    smem = pl.BlockSpec(memory_space=pltpu.SMEM)
    vmem = pl.BlockSpec(memory_space=pltpu.VMEM)
    rows = (tokens // LANES, LANES)
    marks = [pltpu.VMEM((tokens, LANES), jnp.bfloat16)] * 4
    params = pltpu.CompilerParams(vmem_limit_bytes=VMEM)
    struct = lambda *shape: jax.ShapeDtypeStruct(shape, f32)
    own_row, own_col, z_row, p_col, q_col = pl.pallas_call(
        first_kernel,
        out_shape=[struct(*rows), struct(1, tokens), struct(rows[0] // 2, LANES), struct(1, half), struct(1, half)],
        in_specs=[smem] + [vmem] * 5,
        scratch_shapes=marks + [pltpu.VMEM((tokens, LANES), f32), pltpu.VMEM((half, LANES), f32)],
        compiler_params=params,
        name="first",
    )(has_pair, vectors, tags, z1, p1, q1)
    own, z_max, p_max, q_max = pl.pallas_call(
        second_kernel,
        out_shape=[struct(*rows)] * 4,
        in_specs=[smem] + [vmem] * 13,
        scratch_shapes=marks
        + [pltpu.VMEM((tokens, LANES), f32)] * 2
        + [pltpu.VMEM((1, tokens), f32)] * 3,
        compiler_params=params,
        name="second",
    )(has_pair, vectors, tags, z1, p1, q1, z2, p2, q2, own_row, own_col, z_row, p_col, q_col)
    z_back = lax.ppermute(z_max, axes, backwards(layer))
    p_back = lax.ppermute(p_max, axes, backwards(ring))
    q_back = lax.ppermute(q_max, axes, backwards(pair))
    q_back = jnp.where(block % ROUNDS < 2, q_back, NEG)
    best = jnp.maximum(jnp.maximum(own, z_back), jnp.maximum(p_back, q_back))
    return jnp.maximum(prior, best.reshape(tokens))


def solution(mesh):
    spec = P(("slab", "corpus"))
    return jax.shard_map(
        functools.partial(per_device, mesh.shape["slab"], mesh.shape["corpus"]),
        mesh=mesh,
        in_specs=(spec, spec, spec),
        out_specs=spec,
        check_vma=False,
    )
```

```python
import functools

import jax
import jax.numpy as jnp
from jax import lax
from jax.experimental import pallas as pl
from jax.experimental.pallas import tpu as pltpu
from jax.sharding import PartitionSpec as P

ROUNDS = 4
NEG = -1e30
MARK = 2.0**50
LANES = 128
ROWS = 256
VMEM = 24 * 2**20
F32 = jnp.float32
BF16 = jnp.bfloat16


def routes(slabs, count):
    layer, ring, pair, beside = [], [], [], []
    for slab in range(slabs):
        for block in range(count):
            place = block % ROUNDS

            def device(position, slab=slab):
                position = position % count
                return slab * count + (count - 1 - position if slab % 2 else position)

            here, other = device(block), device(count - 1 - block, slab ^ 1)
            layer.append((here, device(block - ROUNDS if place == 0 else block + ROUNDS)))
            ring.append((here, device(block - place + (place + 1) % ROUNDS)))
            pair.append((here, device(block + 2) if place < 2 else other))
            beside.append((here, other))
    return layer, ring, pair, beside


def backwards(pairs):
    return [(target, source) for source, target in pairs]


def struct(*shape, dtype=F32):
    return jax.ShapeDtypeStruct(shape, dtype)


def call(name, kernel, operands, outs, specs=None, scratch=()):
    moved = sum(x.size * x.dtype.itemsize for x in list(operands) + list(outs))
    return pl.pallas_call(
        kernel,
        out_shape=outs,
        in_specs=specs or [pl.BlockSpec(memory_space=pltpu.VMEM)] * len(operands),
        out_specs=[pl.BlockSpec(memory_space=pltpu.VMEM)] * len(outs),
        scratch_shapes=scratch,
        compiler_params=pltpu.CompilerParams(vmem_limit_bytes=VMEM),
        cost_estimate=pl.CostEstimate(flops=0, bytes_accessed=moved, transcendentals=0),
        name=name,
    )(*operands)


def mark(tags, out, value):
    lane = lax.broadcasted_iota(jnp.int32, (LANES, LANES), 0).astype(F32)
    for row in range(tags.shape[0]):
        hit = jnp.where(tags[row : row + 1].astype(F32) == lane, F32(value), F32(0.0))
        out[row * LANES : (row + 1) * LANES] = hit.T.astype(BF16)


def tile(left, left_marks, right, right_marks):
    wide = jnp.concatenate([right, right_marks], axis=1)
    columns = wide.shape[0]
    colmax, rowmax = None, []
    for start in range(0, left.shape[0], ROWS):
        here = slice(start, start + ROWS)
        tall = jnp.concatenate([left[here], left_marks[here]], axis=1)
        scores = lax.dot_general(tall, wide, (((1,), (1,)), ((), ())), preferred_element_type=F32)
        best = scores[:, :LANES]
        for lane in range(LANES, columns, LANES):
            best = jnp.maximum(best, scores[:, lane : lane + LANES])
        rowmax.append(jnp.max(best.reshape(ROWS // LANES, LANES, LANES), axis=2))
        over = jnp.max(scores.reshape(ROWS // 8, 8, columns), axis=0)
        colmax = over if colmax is None else jnp.maximum(colmax, over)
    return jnp.concatenate(rowmax, axis=0), jnp.max(colmax, axis=0, keepdims=True)


def pack(vec, docs, own1, own2, own):
    tokens = vec.shape[0]
    half = tokens // 2
    tags = docs[...].astype(F32).astype(BF16)
    own1[:half] = vec[:half]
    own2[:half] = vec[half:]
    own[:tokens] = vec[...]
    own1[half:] = tags
    own2[half:] = tags
    own[tokens:] = tags


def per_device(slabs, count, vectors, docs, prior):
    axes = ("slab", "corpus")
    tokens, dim = vectors.shape
    half = tokens // 2
    lines = tokens // LANES
    part = lines // 2
    layer, ring, pair, beside = routes(slabs, count)
    block = lax.axis_index("corpus")
    block = jnp.where(lax.axis_index("slab") % 2 == 1, count - 1 - block, block)
    has_pair = (block % ROUNDS >= 2).astype(jnp.int32).reshape(1)
    marks = struct(tokens, LANES, dtype=BF16)
    smem = pl.BlockSpec(memory_space=pltpu.SMEM)
    vmem = pl.BlockSpec(memory_space=pltpu.VMEM)
    whole, piece = struct(lines, LANES), struct(part, LANES)

    own1, own2, own = call(
        "pack",
        pack,
        [vectors, docs.reshape(lines, LANES)],
        [struct(half + lines, dim, dtype=BF16)] * 2 + [struct(tokens + lines, dim, dtype=BF16)],
    )
    p1 = lax.ppermute(own1, axes, ring)
    z1 = lax.ppermute(own1, axes, layer)
    q = lax.ppermute(own, axes, pair)
    p2 = lax.ppermute(own2, axes, ring)
    z2 = lax.ppermute(own2, axes, layer)
    def own_marks(own, out):
        mark(own[tokens:], out, -MARK)

    (own_m,) = call("own_marks", own_marks, [own], [marks])

    def ring1(own, own_m, p1, p_m, own_out, p_out):
        mark(p1[half:], p_m, MARK)
        row, col = tile(own[:tokens], own_m[...], p1[:half], p_m[:half])
        own_out[...] = row
        p_out[...] = col.reshape(part, LANES)

    p_m, own_max, p1_max = call("ring1", ring1, [own, own_m, p1], [marks, whole, piece])

    def layer1(own, own_m, p1, p_m, z1, own_max, p_max, z_m, own_out, p_out, z_out):
        mark(z1[half:], z_m, MARK)
        row1, col1 = tile(z1[:half], -z_m[:half], p1[:half], p_m[:half])
        row2, col2 = tile(z1[:half], z_m[:half], own[:tokens], own_m[...])
        own_out[...] = jnp.maximum(own_max[...], col2.reshape(lines, LANES))
        p_out[...] = jnp.maximum(p_max[...], col1.reshape(part, LANES))
        z_out[...] = jnp.maximum(row1, row2)

    z_m, own_max, p1_max, z1_max = call(
        "layer1", layer1, [own, own_m, p1, p_m, z1, own_max, p1_max], [marks, whole, piece, piece]
    )

    def second(p1, p2, p_m, z1, z2, z_m, z1_max, p1_max, z_out, p_out):
        row1, col1 = tile(z2[:half], -z_m[half:], p1[:half], p_m[:half])
        row2, col2 = tile(z2[:half], -z_m[half:], p2[:half], p_m[half:])
        row3, col3 = tile(z1[:half], -z_m[:half], p2[:half], p_m[half:])
        z_out[:part] = jnp.maximum(z1_max[...], row3)
        z_out[part:] = jnp.maximum(row1, row2)
        p_out[:part] = jnp.maximum(p1_max[...], col1.reshape(part, LANES))
        p_out[part:] = jnp.maximum(col2, col3).reshape(part, LANES)

    z_max, p_max = call("second", second, [p1, p2, p_m, z1, z2, z_m, z1_max, p1_max], [whole, whole])
    swap, z_max = lax.optimization_barrier((q, z_max))
    r = lax.ppermute(swap, axes, beside)

    def ring2(own, own_m, p2, p_m, own_max, p_max, own_out, p_out):
        row, col = tile(own[:tokens], own_m[...], p2[:half], p_m[half:])
        own_out[...] = jnp.maximum(own_max[...], row)
        p_out[:part] = p_max[:part]
        p_out[part:] = jnp.maximum(p_max[part:], col.reshape(part, LANES))

    own_max, p_max = call("ring2", ring2, [own, own_m, p2, p_m, own_max, p_max], [whole, whole])
    p_back = lax.ppermute(p_max, axes, backwards(ring))

    cut = tokens * 3 // 4

    def pairs1(has, z1, z2, z_m, q, r, z_max, after, z_out, row_out, col_out, q_m, r_m):
        mark(q[tokens:], q_m, MARK)

        @pl.when(has[0] > 0)
        def _():
            row1, col1 = tile(z1[:half], -z_m[:half], q[:cut], q_m[:cut])
            row2, col2 = tile(z2[:half], -z_m[half:], q[:cut], q_m[:cut])
            z_out[:part] = jnp.maximum(z_max[:part], row1)
            z_out[part:] = jnp.maximum(z_max[part:], row2)
            row_out[...] = jnp.full((lines, LANES), NEG, F32)
            col_out[...] = jnp.maximum(col1, col2).reshape(cut // LANES, LANES)

        @pl.when(has[0] == 0)
        def _():
            mark(r[tokens:], r_m, -MARK)
            row, col = tile(q[:tokens], q_m[...], r[:cut], r_m[:cut])
            z_out[...] = z_max[...]
            row_out[...] = row
            col_out[...] = col.reshape(cut // LANES, LANES)

    z_max, row_max, col_max, q_m, r_m = call(
        "pairs1",
        pairs1,
        [has_pair, z1, z2, z_m, q, r, z_max, p_max],
        [whole, whole, struct(cut // LANES, LANES), marks, marks],
        specs=[smem] + [vmem] * 7,
    )

    def pairs2(has, z1, z2, z_m, q, q_m, r, r_m, z_max, row_max, col_max, own_max, p_back, z_out, own_out, out):
        own_out[...] = jnp.maximum(own_max[...], p_back[...])
        out[lines : lines + cut // LANES] = col_max[...]

        @pl.when(has[0] > 0)
        def _():
            row1, col1 = tile(z1[:half], -z_m[:half], q[cut:tokens], q_m[cut:])
            row2, col2 = tile(z2[:half], -z_m[half:], q[cut:tokens], q_m[cut:])
            z_out[:part] = jnp.maximum(z_max[:part], row1)
            z_out[part:] = jnp.maximum(z_max[part:], row2)
            out[:lines] = row_max[...]
            out[lines + cut // LANES :] = jnp.maximum(col1, col2).reshape(lines - cut // LANES, LANES)

        @pl.when(has[0] == 0)
        def _():
            row, col = tile(q[:tokens], q_m[...], r[cut:tokens], r_m[cut:])
            z_out[...] = z_max[...]
            out[:lines] = jnp.maximum(row_max[...], row)
            out[lines + cut // LANES :] = col.reshape(lines - cut // LANES, LANES)

    z_max, own_max, mine = call(
        "pairs2",
        pairs2,
        [has_pair, z1, z2, z_m, q, q_m, r, r_m, z_max, row_max, col_max, own_max, p_back],
        [whole, whole, struct(2 * lines, LANES)],
        specs=[smem] + [vmem] * 12,
    )
    theirs = lax.ppermute(mine, axes, beside)

    def layer2(own, own_m, z2, z_m, own_max, z_max, own_out, z_out):
        row, col = tile(z2[:half], z_m[half:], own[:tokens], own_m[...])
        own_out[...] = jnp.maximum(own_max[...], col.reshape(lines, LANES))
        z_out[:part] = z_max[:part]
        z_out[part:] = jnp.maximum(z_max[part:], row)

    own_max, z_max = call(
        "layer2", layer2, [own, own_m, z2, z_m, own_max, z_max], [whole, whole]
    )
    z_back = lax.ppermute(z_max, axes, backwards(layer))

    def merge(has, mine, theirs, own_max, own_out, q_out):
        got = jnp.where(has[0] > 0, theirs[...], F32(NEG))
        own_out[...] = jnp.maximum(own_max[...], got[:lines])
        q_out[...] = jnp.maximum(mine[lines:], got[lines:])

    own_max, q_max = call(
        "merge", merge, [has_pair, mine, theirs, own_max], [whole, whole], specs=[smem] + [vmem] * 3
    )
    q_back = lax.ppermute(q_max, axes, backwards(pair))
    q_back = jnp.where(has_pair > 0, NEG, q_back)
    best = jnp.maximum(jnp.maximum(own_max, z_back), q_back)
    return jnp.maximum(prior, best.reshape(tokens))


def solution(mesh):
    spec = P(("slab", "corpus"))
    return jax.shard_map(
        functools.partial(per_device, mesh.shape["slab"], mesh.shape["corpus"]),
        mesh=mesh,
        in_specs=(spec, spec, spec),
        out_specs=spec,
        check_vma=False,
    )
```

```python
import functools

import jax
import jax.numpy as jnp
from jax import lax
from jax.experimental import pallas as pl
from jax.experimental.pallas import tpu as pltpu
from jax.sharding import PartitionSpec as P

ROUNDS = 4
NEG = -1e30
MARK = 2.0**50
LANES = 128
ROWS = 256
VMEM = 24 * 2**20
F32 = jnp.float32
BF16 = jnp.bfloat16
HEAD = 10


def routes(slabs, count):
    layer, ring, pair, beside = [], [], [], []
    for slab in range(slabs):
        for block in range(count):
            place = block % ROUNDS

            def device(position, slab=slab):
                position = position % count
                return slab * count + (count - 1 - position if slab % 2 else position)

            here, other = device(block), device(count - 1 - block, slab ^ 1)
            layer.append((here, device(block - ROUNDS if place == 0 else block + ROUNDS)))
            ring.append((here, device(block - place + (place + 1) % ROUNDS)))
            pair.append((here, device(block + 2) if place < 2 else other))
            beside.append((here, other))
    return layer, ring, pair, beside


def backwards(pairs):
    return [(target, source) for source, target in pairs]


def struct(*shape, dtype=F32):
    return jax.ShapeDtypeStruct(shape, dtype)


def call(name, kernel, operands, outs, specs=None, scratch=()):
    moved = sum(x.size * x.dtype.itemsize for x in list(operands) + list(outs))
    return pl.pallas_call(
        kernel,
        out_shape=outs,
        in_specs=specs or [pl.BlockSpec(memory_space=pltpu.VMEM)] * len(operands),
        out_specs=[pl.BlockSpec(memory_space=pltpu.VMEM)] * len(outs),
        scratch_shapes=scratch,
        compiler_params=pltpu.CompilerParams(vmem_limit_bytes=VMEM),
        cost_estimate=pl.CostEstimate(flops=0, bytes_accessed=moved, transcendentals=0),
        name=name,
    )(*operands)


def mark(tags, out, value):
    lane = lax.broadcasted_iota(jnp.int32, (LANES, LANES), 0).astype(F32)
    for row in range(tags.shape[0]):
        hit = jnp.where(tags[row : row + 1].astype(F32) == lane, F32(value), F32(0.0))
        out[row * LANES : (row + 1) * LANES] = hit.T.astype(BF16)


def tile(lefts, rights):
    wide = jnp.concatenate([jnp.concatenate(pair, axis=1) for pair in rights], axis=0)
    columns = wide.shape[0]
    colmax, rowmax = None, []
    for left, left_marks in lefts:
        for start in range(0, left.shape[0], ROWS):
            here = slice(start, start + ROWS)
            tall = jnp.concatenate([left[here], left_marks[here]], axis=1)
            scores = lax.dot_general(tall, wide, (((1,), (1,)), ((), ())), preferred_element_type=F32)
            best = scores[:, :LANES]
            for lane in range(LANES, columns, LANES):
                best = jnp.maximum(best, scores[:, lane : lane + LANES])
            rowmax.append(jnp.max(best.reshape(ROWS // LANES, LANES, LANES), axis=2))
            over = jnp.max(scores.reshape(ROWS // 8, 8, columns), axis=0)
            colmax = over if colmax is None else jnp.maximum(colmax, over)
    return jnp.concatenate(rowmax, axis=0), jnp.max(colmax, axis=0).reshape(columns // LANES, LANES)


def pack(vec, docs, own1, own2, own):
    tokens = vec.shape[0]
    head = own1.shape[0] - docs.shape[0]
    tags = docs[...].astype(F32).astype(BF16)
    own1[:head] = vec[:head]
    own1[head:] = tags
    own2[...] = vec[head:]
    own[:tokens] = vec[...]
    own[tokens:] = tags


def after(value, *others):
    return lax.optimization_barrier((value, *others))[0]


def per_device(slabs, count, vectors, docs, prior):
    axes = ("slab", "corpus")
    tokens, dim = vectors.shape
    lines = tokens // LANES
    head = tokens * HEAD // 16
    part = head // LANES
    rest = lines - part
    layer, ring, pair, beside = routes(slabs, count)
    block = lax.axis_index("corpus")
    block = jnp.where(lax.axis_index("slab") % 2 == 1, count - 1 - block, block)
    has_pair = (block % ROUNDS >= 2).astype(jnp.int32).reshape(1)
    marks = struct(tokens, LANES, dtype=BF16)
    smem = pl.BlockSpec(memory_space=pltpu.SMEM)
    vmem = pl.BlockSpec(memory_space=pltpu.VMEM)
    whole, piece1, piece2 = struct(lines, LANES), struct(part, LANES), struct(rest, LANES)

    own1, own2, own = call(
        "pack",
        pack,
        [vectors, docs.reshape(lines, LANES)],
        [struct(rows, dim, dtype=BF16) for rows in (head + lines, tokens - head, tokens + lines)],
    )
    p1 = lax.ppermute(own1, axes, ring)
    z1 = lax.ppermute(own1, axes, layer)
    q = lax.ppermute(own, axes, pair)
    p2 = lax.ppermute(own2, axes, ring)
    z2 = lax.ppermute(own2, axes, layer)

    def own_marks(own, out):
        mark(own[tokens:], out, -MARK)

    (own_m,) = call("own_marks", own_marks, [own], [marks])

    def ring1(own, own_m, p1, p_m, own_out, p_out):
        mark(p1[head:], p_m, MARK)
        p_out[...], own_out[...] = tile([(p1[:head], p_m[:head])], [(own[:tokens], own_m[...])])

    p_m, own_max, p1_max = call("ring1", ring1, [own, own_m, p1], [marks, whole, piece1])

    def layer1(own, own_m, p1, p_m, z1, own_max, p_max, z_m, own_out, p_out, z_out):
        mark(z1[head:], z_m, MARK)
        row, col = tile([(z1[:head], z_m[:head])], [(own[:tokens], own_m[...]), (p1[:head], -p_m[:head])])
        own_out[...] = jnp.maximum(own_max[...], col[:lines])
        p_out[...] = jnp.maximum(p_max[...], col[lines:])
        z_out[...] = row

    z_m, own_max, p1_max, z1_max = call(
        "layer1", layer1, [own, own_m, p1, p_m, z1, own_max, p1_max], [marks, whole, piece1, piece1]
    )

    def second(p1, p2, p_m, z1, z2, z_m, z1_max, p1_max, z_out, p_out):
        row1, col1 = tile([(z2[...], -z_m[head:])], [(p1[:head], p_m[:head]), (p2[...], p_m[head:])])
        row2, col2 = tile([(p2[...], -p_m[head:])], [(z1[:head], z_m[:head])])
        z_out[:part] = jnp.maximum(z1_max[...], col2)
        z_out[part:] = row1
        p_out[:part] = jnp.maximum(p1_max[...], col1[:part])
        p_out[part:] = jnp.maximum(col1[part:], row2)

    z_max, p_max = call("second", second, [p1, p2, p_m, z1, z2, z_m, z1_max, p1_max], [whole, whole])
    r = lax.ppermute(after(q, z_max), axes, beside)

    def ring2(own, own_m, p2, p_m, own_max, p_max, own_out, p_out):
        row, col = tile([(p2[...], p_m[head:])], [(own[:tokens], own_m[...])])
        own_out[...] = jnp.maximum(own_max[...], col)
        p_out[:part] = p_max[:part]
        p_out[part:lines] = jnp.maximum(p_max[part:], row)
        p_out[lines:] = jnp.full((3 * lines, LANES), NEG, F32)

    own_max, p_max = call(
        "ring2", ring2, [own, own_m, p2, p_m, own_max, p_max], [whole, struct(4 * lines, LANES)]
    )
    p_back = lax.ppermute(p_max, axes, backwards(ring))

    def pairs(has, z1, z2, z_m, q, r, z_max, after, z_out, out, q_m, r_m):
        mark(q[tokens:], q_m, MARK)

        @pl.when(has[0] > 0)
        def _():
            row, col = tile([(z1[:head], -z_m[:head]), (z2[...], -z_m[head:])], [(q[:tokens], q_m[...])])
            z_out[...] = jnp.maximum(z_max[...], row)
            out[:lines] = jnp.full((lines, LANES), NEG, F32)
            out[lines:] = col

        @pl.when(has[0] == 0)
        def _():
            mark(r[tokens:], r_m, -MARK)
            z_out[...] = z_max[...]
            out[:lines], out[lines:] = tile([(q[:tokens], q_m[...])], [(r[:tokens], r_m[...])])

    z_max, mine = call(
        "pairs",
        pairs,
        [has_pair, z1, z2, z_m, q, r, z_max, p_max],
        [whole, struct(2 * lines, LANES)],
        specs=[smem] + [vmem] * 7,
        scratch=[pltpu.VMEM((tokens, LANES), BF16)] * 2,
    )
    theirs = lax.ppermute(mine, axes, beside)

    def layer2(own, own_m, z2, z_m, own_max, z_max, own_out, z_out):
        row, col = tile([(z2[...], z_m[head:])], [(own[:tokens], own_m[...])])
        own_out[...] = jnp.maximum(own_max[...], col)
        z_out[:part] = z_max[:part]
        z_out[part:] = jnp.maximum(z_max[part:], row)

    own_max, z_max = call("layer2", layer2, [own, own_m, z2, z_m, own_max, z_max], [whole, whole])
    z_back = lax.ppermute(z_max, axes, backwards(layer))

    def merge(has, mine, theirs, own_max, p_back, own_out, q_out):
        got = jnp.where(has[0] > 0, theirs[...], F32(NEG))
        own_out[...] = jnp.maximum(jnp.maximum(own_max[...], p_back[:lines]), got[:lines])
        q_out[...] = jnp.maximum(mine[lines:], got[lines:])

    own_max, q_max = call(
        "merge", merge, [has_pair, mine, theirs, own_max, p_back], [whole, whole], specs=[smem] + [vmem] * 4
    )
    q_back = lax.ppermute(q_max, axes, backwards(pair))
    q_back = jnp.where(has_pair > 0, NEG, q_back)
    best = jnp.maximum(jnp.maximum(own_max, z_back), q_back)
    return jnp.maximum(prior, best.reshape(tokens))


def solution(mesh):
    spec = P(("slab", "corpus"))
    return jax.shard_map(
        functools.partial(per_device, mesh.shape["slab"], mesh.shape["corpus"]),
        mesh=mesh,
        in_specs=(spec, spec, spec),
        out_specs=spec,
        check_vma=False,
    )
```

```python
import functools

import jax
import jax.numpy as jnp
from jax import lax
from jax.experimental import pallas as pl
from jax.experimental.pallas import tpu as pltpu
from jax.sharding import PartitionSpec as P

ROUNDS = 4
NEG = -1e30
MARK = 2.0**50
LANES = 128
ROWS = 512
VMEM = 24 * 2**20
F32 = jnp.float32
BF16 = jnp.bfloat16
HEAD = 10


def routes(slabs, count):
    layer, ring, pair, beside = [], [], [], []
    for slab in range(slabs):
        for block in range(count):
            place = block % ROUNDS

            def device(position, slab=slab):
                position = position % count
                return slab * count + (count - 1 - position if slab % 2 else position)

            here, other = device(block), device(count - 1 - block, slab ^ 1)
            layer.append((here, device(block - ROUNDS if place == 0 else block + ROUNDS)))
            ring.append((here, device(block - place + (place + 1) % ROUNDS)))
            pair.append((here, device(block + 2) if place < 2 else other))
            beside.append((here, other))
    return layer, ring, pair, beside


def backwards(pairs):
    return [(target, source) for source, target in pairs]


def struct(*shape, dtype=F32):
    return jax.ShapeDtypeStruct(shape, dtype)


def call(name, kernel, operands, outs, specs=None, scratch=()):
    moved = sum(x.size * x.dtype.itemsize for x in list(operands) + list(outs))
    return pl.pallas_call(
        kernel,
        out_shape=outs,
        in_specs=specs or [pl.BlockSpec(memory_space=pltpu.VMEM)] * len(operands),
        out_specs=[pl.BlockSpec(memory_space=pltpu.VMEM)] * len(outs),
        scratch_shapes=scratch,
        compiler_params=pltpu.CompilerParams(vmem_limit_bytes=VMEM),
        cost_estimate=pl.CostEstimate(flops=0, bytes_accessed=moved, transcendentals=0),
        name=name,
    )(*operands)


def mark(tags, out, value):
    lane = lax.broadcasted_iota(jnp.int32, (LANES, LANES), 0).astype(F32)
    for row in range(tags.shape[0]):
        hit = jnp.where(tags[row : row + 1].astype(F32) == lane, F32(value), F32(0.0))
        out[row * LANES : (row + 1) * LANES] = hit.T.astype(BF16)


def tile(lefts, rights):
    wide = jnp.concatenate([jnp.concatenate(pair, axis=1) for pair in rights], axis=0)
    columns = wide.shape[0]
    colmax, rowmax = None, []
    for left, left_marks in lefts:
        count = left.shape[0] // LANES
        pieces = -(-count * LANES // ROWS)
        for piece in range(pieces):
            here = slice(piece * count // pieces * LANES, (piece + 1) * count // pieces * LANES)
            size = here.stop - here.start
            tall = jnp.concatenate([left[here], left_marks[here]], axis=1)
            scores = lax.dot_general(tall, wide, (((1,), (1,)), ((), ())), preferred_element_type=F32)
            best = scores[:, :LANES]
            for lane in range(LANES, columns, LANES):
                best = jnp.maximum(best, scores[:, lane : lane + LANES])
            rowmax.append(jnp.max(best.reshape(size // LANES, LANES, LANES), axis=2))
            over = jnp.max(scores.reshape(size // 8, 8, columns), axis=0)
            colmax = over if colmax is None else jnp.maximum(colmax, over)
    return jnp.concatenate(rowmax, axis=0), jnp.max(colmax, axis=0).reshape(columns // LANES, LANES)


def pack(vec, docs, own1, own2, own):
    tokens = vec.shape[0]
    head = own1.shape[0] - docs.shape[0]
    tags = docs[...].astype(F32).astype(BF16)
    own1[:head] = vec[:head]
    own1[head:] = tags
    own2[...] = vec[head:]
    own[:tokens] = vec[...]
    own[tokens:] = tags


def after(value, *others):
    return lax.optimization_barrier((value, *others))[0]


def per_device(slabs, count, vectors, docs, prior):
    axes = ("slab", "corpus")
    tokens, dim = vectors.shape
    lines = tokens // LANES
    head = tokens * HEAD // 16
    part = head // LANES
    rest = lines - part
    layer, ring, pair, beside = routes(slabs, count)
    block = lax.axis_index("corpus")
    block = jnp.where(lax.axis_index("slab") % 2 == 1, count - 1 - block, block)
    has_pair = (block % ROUNDS >= 2).astype(jnp.int32).reshape(1)
    far = jnp.where(block % ROUNDS == 0, block == count - ROUNDS, block < ROUNDS).astype(jnp.int32).reshape(1)
    marks = struct(tokens, LANES, dtype=BF16)
    marks1, marks2 = struct(head, LANES, dtype=BF16), struct(tokens - head, LANES, dtype=BF16)
    smem = pl.BlockSpec(memory_space=pltpu.SMEM)
    vmem = pl.BlockSpec(memory_space=pltpu.VMEM)
    whole, piece1, piece2 = struct(lines, LANES), struct(part, LANES), struct(rest, LANES)

    own1, own2, own = call(
        "pack",
        pack,
        [vectors, docs.reshape(lines, LANES)],
        [struct(rows, dim, dtype=BF16) for rows in (head + lines, tokens - head, tokens + lines)],
    )
    p1 = lax.ppermute(own1, axes, ring)
    z1 = lax.ppermute(own1, axes, layer)
    q = lax.ppermute(own, axes, pair)
    p2 = lax.ppermute(own2, axes, ring)
    z2 = lax.ppermute(own2, axes, layer)

    def own_marks(own, out):
        mark(own[tokens:], out, -MARK)

    (own_m,) = call("own_marks", own_marks, [own], [marks])

    def ring1(own, own_m, p1, p_m1, p_m2, own_out, p_out):
        mark(p1[head : head + part], p_m1, MARK)
        mark(p1[head + part :], p_m2, MARK)
        p_out[...], own_out[...] = tile([(p1[:head], p_m1[...])], [(own[:tokens], own_m[...])])

    p_m1, p_m2, own_max, p1_max = call("ring1", ring1, [own, own_m, p1], [marks1, marks2, whole, piece1])

    def layer1(own, own_m, p1, p_m1, z1, own_max, p_max, z_m1, z_m2, own_out, p_out, z_out):
        mark(z1[head : head + part], z_m1, MARK)
        mark(z1[head + part :], z_m2, MARK)
        row, col = tile([(z1[:head], z_m1[...])], [(own[:tokens], own_m[...]), (p1[:head], -p_m1[...])])
        own_out[...] = jnp.maximum(own_max[...], col[:lines])
        p_out[...] = jnp.maximum(p_max[...], col[lines:])
        z_out[...] = row

    z_m1, z_m2, own_max, p1_max, z1_max = call(
        "layer1",
        layer1,
        [own, own_m, p1, p_m1, z1, own_max, p1_max],
        [marks1, marks2, whole, piece1, piece1],
    )

    def second(p1, p_m1, p2, p_m2, z1, z_m1, z2, z_m2, z1_max, p1_max, z_out, p_out):
        row1, col1 = tile([(z2[...], -z_m2[...])], [(p1[:head], p_m1[...]), (p2[...], p_m2[...])])
        row2, col2 = tile([(p2[...], -p_m2[...])], [(z1[:head], z_m1[...])])
        z_out[:part] = jnp.maximum(z1_max[...], col2)
        z_out[part:] = row1
        p_out[:part] = jnp.maximum(p1_max[...], col1[:part])
        p_out[part:] = jnp.maximum(col1[part:], row2)

    z_max, p_max = call(
        "second", second, [p1, p_m1, p2, p_m2, z1, z_m1, z2, z_m2, z1_max, p1_max], [whole, whole]
    )
    r = lax.ppermute(after(q, z_max), axes, beside)

    def layer2(own, own_m, z2, z_m2, own_max, z_max, own_out, z_out):
        row, col = tile([(z2[...], z_m2[...])], [(own[:tokens], own_m[...])])
        own_out[...] = jnp.maximum(own_max[...], col)
        z_out[:part] = z_max[:part]
        z_out[part:] = jnp.maximum(z_max[part:], row)

    own_max, z_max = call("layer2", layer2, [own, own_m, z2, z_m2, own_max, z_max], [whole, whole])

    def pairs(has, z1, z2, q, r, z_max, z_out, out, q_m, other_m):
        mark(q[tokens:], q_m, MARK)
        z_out[lines:] = jnp.full((3 * lines, LANES), NEG, F32)

        @pl.when(has[0] > 0)
        def _():
            mark(z1[head:], other_m, -MARK)
            row, col = tile([(z1[:head], other_m[:head]), (z2[...], other_m[head:])], [(q[:tokens], q_m[...])])
            z_out[:lines] = jnp.maximum(z_max[...], row)
            out[:lines] = jnp.full((lines, LANES), NEG, F32)
            out[lines:] = col

        @pl.when(has[0] == 0)
        def _():
            mark(r[tokens:], other_m, -MARK)
            z_out[:lines] = z_max[...]
            out[:lines], out[lines:] = tile([(q[:tokens], q_m[...])], [(r[:tokens], other_m[...])])

    z_max, mine = call(
        "pairs",
        pairs,
        [has_pair, z1, z2, q, r, z_max],
        [struct(4 * lines, LANES), struct(2 * lines, LANES)],
        specs=[smem] + [vmem] * 5,
        scratch=[pltpu.VMEM((tokens, LANES), BF16)] * 2,
    )
    theirs = lax.ppermute(mine, axes, beside)

    def ring2(wanted, far, own, own_m, p2, p_m2, own_max, p_max, own_out, p_out):
        @pl.when(far[0] == wanted)
        def _():
            row, col = tile([(p2[...], p_m2[...])], [(own[:tokens], own_m[...])])
            own_out[...] = jnp.maximum(own_max[...], col)
            p_out[:part] = p_max[:part]
            p_out[part:] = jnp.maximum(p_max[part:], row)

        @pl.when(far[0] != wanted)
        def _():
            own_out[...] = own_max[...]
            p_out[...] = p_max[...]

    p_max = after(p_max, mine)
    for wanted in (1, 0):
        own_max, p_max = call(
            "ring2",
            functools.partial(ring2, wanted),
            [far, own, own_m, p2, p_m2, own_max, p_max],
            [whole, whole],
            specs=[smem] + [vmem] * 6,
        )
        if wanted:
            z_back = lax.ppermute(after(z_max, p_max), axes, backwards(layer))
    p_back = lax.ppermute(p_max, axes, backwards(ring))

    def merge(has, mine, theirs, own_max, own_out, q_out):
        got = jnp.where(has[0] > 0, theirs[...], F32(NEG))
        own_out[...] = jnp.maximum(own_max[...], got[:lines])
        q_out[...] = jnp.maximum(mine[lines:], got[lines:])

    own_max, q_max = call(
        "merge", merge, [has_pair, mine, theirs, own_max], [whole, whole], specs=[smem] + [vmem] * 3
    )
    q_back = lax.ppermute(q_max, axes, backwards(pair))
    q_back = jnp.where(has_pair > 0, NEG, q_back)
    best = jnp.maximum(jnp.maximum(own_max, z_back[:lines]), jnp.maximum(p_back, q_back))
    return jnp.maximum(prior, best.reshape(tokens))


def solution(mesh):
    spec = P(("slab", "corpus"))
    return jax.shard_map(
        functools.partial(per_device, mesh.shape["slab"], mesh.shape["corpus"]),
        mesh=mesh,
        in_specs=(spec, spec, spec),
        out_specs=spec,
        check_vma=False,
    )
```

```python
import functools

import jax
import jax.numpy as jnp
from jax import lax
from jax.experimental import pallas as pl
from jax.experimental.pallas import tpu as pltpu
from jax.sharding import PartitionSpec as P

ROUNDS = 4
NEG = -1e30
MARK = 2.0**50
LANES = 128
ROWS = 512
VMEM = 24 * 2**20
F32 = jnp.float32
BF16 = jnp.bfloat16
HEAD = 10


def routes(slabs, count):
    layer, ring, pair, beside = [], [], [], []
    for slab in range(slabs):
        for block in range(count):
            place = block % ROUNDS

            def device(position, slab=slab):
                position = position % count
                return slab * count + (count - 1 - position if slab % 2 else position)

            here, other = device(block), device(count - 1 - block, slab ^ 1)
            layer.append((here, device(block - ROUNDS if place == 0 else block + ROUNDS)))
            ring.append((here, device(block - place + (place + 1) % ROUNDS)))
            pair.append((here, device(block + 2) if place < 2 else other))
            beside.append((here, other))
    return layer, ring, pair, beside


def backwards(pairs):
    return [(target, source) for source, target in pairs]


def struct(*shape, dtype=F32):
    return jax.ShapeDtypeStruct(shape, dtype)


def call(name, kernel, operands, outs, specs=None, scratch=()):
    moved = sum(x.size * x.dtype.itemsize for x in list(operands) + list(outs))
    return pl.pallas_call(
        kernel,
        out_shape=outs,
        in_specs=specs or [pl.BlockSpec(memory_space=pltpu.VMEM)] * len(operands),
        out_specs=[pl.BlockSpec(memory_space=pltpu.VMEM)] * len(outs),
        scratch_shapes=scratch,
        compiler_params=pltpu.CompilerParams(vmem_limit_bytes=VMEM),
        cost_estimate=pl.CostEstimate(flops=0, bytes_accessed=moved, transcendentals=0),
        name=name,
    )(*operands)


def mark(tags, out, value):
    lane = lax.broadcasted_iota(jnp.int32, (LANES, LANES), 0).astype(F32)
    for row in range(tags.shape[0]):
        hit = jnp.where(tags[row : row + 1].astype(F32) == lane, F32(value), F32(0.0))
        out[row * LANES : (row + 1) * LANES] = hit.T.astype(BF16)


def tile(lefts, rights):
    wide = jnp.concatenate([jnp.concatenate(pair, axis=1) for pair in rights], axis=0)
    columns = wide.shape[0]
    colmax, rowmax = None, []
    for left, left_marks in lefts:
        count = left.shape[0] // LANES
        pieces = -(-count * LANES // ROWS)
        for piece in range(pieces):
            here = slice(piece * count // pieces * LANES, (piece + 1) * count // pieces * LANES)
            size = here.stop - here.start
            tall = jnp.concatenate([left[here], left_marks[here]], axis=1)
            scores = lax.dot_general(tall, wide, (((1,), (1,)), ((), ())), preferred_element_type=F32)
            best = scores[:, :LANES]
            for lane in range(LANES, columns, LANES):
                best = jnp.maximum(best, scores[:, lane : lane + LANES])
            rowmax.append(jnp.max(best.reshape(size // LANES, LANES, LANES), axis=2))
            over = jnp.max(scores.reshape(size // 8, 8, columns), axis=0)
            colmax = over if colmax is None else jnp.maximum(colmax, over)
    return jnp.concatenate(rowmax, axis=0), jnp.max(colmax, axis=0).reshape(columns // LANES, LANES)


def pack(vec, docs, own1, own2, own):
    tokens = vec.shape[0]
    head = own1.shape[0] - docs.shape[0]
    tags = docs[...].astype(F32).astype(BF16)
    own1[:head] = vec[:head]
    own1[head:] = tags
    own2[...] = vec[head:]
    own[:tokens] = vec[...]
    own[tokens:] = tags


def after(value, *others):
    return lax.optimization_barrier((value, *others))[0]


def per_device(slabs, count, vectors, docs, prior):
    axes = ("slab", "corpus")
    tokens, dim = vectors.shape
    lines = tokens // LANES
    head = tokens * HEAD // 16
    part = head // LANES
    rest = lines - part
    layer, ring, pair, beside = routes(slabs, count)
    block = lax.axis_index("corpus")
    block = jnp.where(lax.axis_index("slab") % 2 == 1, count - 1 - block, block)
    has_pair = (block % ROUNDS >= 2).astype(jnp.int32).reshape(1)
    far = jnp.where(block % ROUNDS == 0, block == count - ROUNDS, block < ROUNDS)
    far = (far & (lax.axis_index("corpus") < ROUNDS)).astype(jnp.int32).reshape(1)
    marks = struct(tokens, LANES, dtype=BF16)
    marks1, marks2 = struct(head, LANES, dtype=BF16), struct(tokens - head, LANES, dtype=BF16)
    smem = pl.BlockSpec(memory_space=pltpu.SMEM)
    vmem = pl.BlockSpec(memory_space=pltpu.VMEM)
    whole, piece1, piece2 = struct(lines, LANES), struct(part, LANES), struct(rest, LANES)

    own1, own2, own = call(
        "pack",
        pack,
        [vectors, docs.reshape(lines, LANES)],
        [struct(rows, dim, dtype=BF16) for rows in (head + lines, tokens - head, tokens + lines)],
    )
    p1 = lax.ppermute(own1, axes, ring)
    z1 = lax.ppermute(own1, axes, layer)
    q = lax.ppermute(own, axes, pair)
    p2 = lax.ppermute(own2, axes, ring)
    z2 = lax.ppermute(own2, axes, layer)

    def own_marks(own, out):
        mark(own[tokens:], out, -MARK)

    (own_m,) = call("own_marks", own_marks, [own], [marks])

    def ring1(own, own_m, p1, p_m1, p_m2, own_out, p_out):
        mark(p1[head : head + part], p_m1, MARK)
        mark(p1[head + part :], p_m2, MARK)
        p_out[...], own_out[...] = tile([(p1[:head], p_m1[...])], [(own[:tokens], own_m[...])])

    p_m1, p_m2, own_max, p1_max = call("ring1", ring1, [own, own_m, p1], [marks1, marks2, whole, piece1])

    def layer1(own, own_m, p1, p_m1, z1, own_max, p_max, z_m1, z_m2, own_out, p_out, z_out):
        mark(z1[head : head + part], z_m1, MARK)
        mark(z1[head + part :], z_m2, MARK)
        row, col = tile([(z1[:head], z_m1[...])], [(own[:tokens], own_m[...]), (p1[:head], -p_m1[...])])
        own_out[...] = jnp.maximum(own_max[...], col[:lines])
        p_out[...] = jnp.maximum(p_max[...], col[lines:])
        z_out[...] = row

    z_m1, z_m2, own_max, p1_max, z1_max = call(
        "layer1",
        layer1,
        [own, own_m, p1, p_m1, z1, own_max, p1_max],
        [marks1, marks2, whole, piece1, piece1],
    )

    def second(p1, p_m1, p2, p_m2, z1, z_m1, z2, z_m2, z1_max, p1_max, z_out, p_out):
        row1, col1 = tile([(z2[...], -z_m2[...])], [(p1[:head], p_m1[...]), (p2[...], p_m2[...])])
        row2, col2 = tile([(p2[...], -p_m2[...])], [(z1[:head], z_m1[...])])
        z_out[:part] = jnp.maximum(z1_max[...], col2)
        z_out[part:] = row1
        p_out[:part] = jnp.maximum(p1_max[...], col1[:part])
        p_out[part:] = jnp.maximum(col1[part:], row2)

    z_max, p_max = call(
        "second", second, [p1, p_m1, p2, p_m2, z1, z_m1, z2, z_m2, z1_max, p1_max], [whole, whole]
    )
    r = lax.ppermute(after(q, z_max), axes, beside)

    def layer2(own, own_m, z2, z_m2, own_max, z_max, own_out, z_out):
        row, col = tile([(z2[...], z_m2[...])], [(own[:tokens], own_m[...])])
        own_out[...] = jnp.maximum(own_max[...], col)
        z_out[:part] = z_max[:part]
        z_out[part:] = jnp.maximum(z_max[part:], row)

    own_max, z_max = call("layer2", layer2, [own, own_m, z2, z_m2, own_max, z_max], [whole, whole])

    def q_marks(q, after, out):
        mark(q[tokens:], out, MARK)

    (q_m,) = call("q_marks", q_marks, [q, own_max], [marks])

    def pairs(has, z1, z2, q, q_m, r, z_max, z_out, out, other_m):
        z_out[lines:] = jnp.full((3 * lines, LANES), NEG, F32)

        @pl.when(has[0] > 0)
        def _():
            mark(z1[head:], other_m, -MARK)
            row, col = tile([(z1[:head], other_m[:head]), (z2[...], other_m[head:])], [(q[:tokens], q_m[...])])
            z_out[:lines] = jnp.maximum(z_max[...], row)
            out[:lines] = jnp.full((lines, LANES), NEG, F32)
            out[lines:] = col

        @pl.when(has[0] == 0)
        def _():
            mark(r[tokens:], other_m, -MARK)
            z_out[:lines] = z_max[...]
            out[:lines], out[lines:] = tile([(q[:tokens], q_m[...])], [(r[:tokens], other_m[...])])

    z_max, mine = call(
        "pairs",
        pairs,
        [has_pair, z1, z2, q, q_m, r, z_max],
        [struct(4 * lines, LANES), struct(2 * lines, LANES)],
        specs=[smem] + [vmem] * 6,
        scratch=[pltpu.VMEM((tokens, LANES), BF16)],
    )
    theirs = lax.ppermute(mine, axes, beside)

    def ring2(wanted, far, own, own_m, p2, p_m2, own_max, p_max, own_out, p_out):
        @pl.when(far[0] == wanted)
        def _():
            row, col = tile([(p2[...], p_m2[...])], [(own[:tokens], own_m[...])])
            own_out[...] = jnp.maximum(own_max[...], col)
            p_out[:part] = p_max[:part]
            p_out[part:] = jnp.maximum(p_max[part:], row)

        @pl.when(far[0] != wanted)
        def _():
            own_out[...] = own_max[...]
            p_out[...] = p_max[...]

    p_max = after(p_max, mine)
    for wanted in (1, 0):
        own_max, p_max = call(
            "ring2",
            functools.partial(ring2, wanted),
            [far, own, own_m, p2, p_m2, own_max, p_max],
            [whole, whole],
            specs=[smem] + [vmem] * 6,
        )
        if wanted:
            z_back = lax.ppermute(after(z_max, p_max), axes, backwards(layer))
    p_back = lax.ppermute(p_max, axes, backwards(ring))

    def merge(has, mine, theirs, own_max, own_out, q_out):
        got = jnp.where(has[0] > 0, theirs[...], F32(NEG))
        own_out[...] = jnp.maximum(own_max[...], got[:lines])
        q_out[...] = jnp.maximum(mine[lines:], got[lines:])

    own_max, q_max = call(
        "merge", merge, [has_pair, mine, theirs, own_max], [whole, whole], specs=[smem] + [vmem] * 3
    )
    q_back = lax.ppermute(q_max, axes, backwards(pair))
    q_back = jnp.where(has_pair > 0, NEG, q_back)
    best = jnp.maximum(jnp.maximum(own_max, z_back[:lines]), jnp.maximum(p_back, q_back))
    return jnp.maximum(prior, best.reshape(tokens))


def solution(mesh):
    spec = P(("slab", "corpus"))
    return jax.shard_map(
        functools.partial(per_device, mesh.shape["slab"], mesh.shape["corpus"]),
        mesh=mesh,
        in_specs=(spec, spec, spec),
        out_specs=spec,
        check_vma=False,
    )
```

```python
import functools

import jax
import jax.numpy as jnp
from jax import lax
from jax.experimental import pallas as pl
from jax.experimental.pallas import tpu as pltpu
from jax.sharding import PartitionSpec as P

ROUNDS = 4
NEG = -1e30
MARK = 2.0**50
LANES = 128
ROWS = 512
VMEM = 24 * 2**20
F32 = jnp.float32
BF16 = jnp.bfloat16
HEAD = 10


def routes(slabs, count):
    layer, ring, pair, beside = [], [], [], []
    for slab in range(slabs):
        for block in range(count):
            place = block % ROUNDS

            def device(position, slab=slab):
                position = position % count
                return slab * count + (count - 1 - position if slab % 2 else position)

            here, other = device(block), device(count - 1 - block, slab ^ 1)
            layer.append((here, device(block - ROUNDS if place == 0 else block + ROUNDS)))
            ring.append((here, device(block - place + (place + 1) % ROUNDS)))
            pair.append((here, device(block + 2) if place < 2 else other))
            beside.append((here, other))
    return layer, ring, pair, beside


def backwards(pairs):
    return [(target, source) for source, target in pairs]


def struct(*shape, dtype=F32):
    return jax.ShapeDtypeStruct(shape, dtype)


def call(name, kernel, operands, outs, specs=None, scratch=()):
    moved = sum(x.size * x.dtype.itemsize for x in list(operands) + list(outs))
    return pl.pallas_call(
        kernel,
        out_shape=outs,
        in_specs=specs or [pl.BlockSpec(memory_space=pltpu.VMEM)] * len(operands),
        out_specs=[pl.BlockSpec(memory_space=pltpu.VMEM)] * len(outs),
        scratch_shapes=scratch,
        compiler_params=pltpu.CompilerParams(vmem_limit_bytes=VMEM),
        cost_estimate=pl.CostEstimate(flops=0, bytes_accessed=moved, transcendentals=0),
        name=name,
    )(*operands)


def mark(tags, out, value):
    lane = lax.broadcasted_iota(jnp.int32, (LANES, LANES), 0).astype(F32)
    for row in range(tags.shape[0]):
        hit = jnp.where(tags[row : row + 1].astype(F32) == lane, F32(value), F32(0.0))
        out[row * LANES : (row + 1) * LANES] = hit.T.astype(BF16)


def tile(lefts, rights):
    wide = jnp.concatenate([jnp.concatenate(pair, axis=1) for pair in rights], axis=0)
    columns = wide.shape[0]
    colmax, rowmax = None, []
    for left, left_marks in lefts:
        count = left.shape[0] // LANES
        pieces = -(-count * LANES // ROWS)
        for piece in range(pieces):
            here = slice(piece * count // pieces * LANES, (piece + 1) * count // pieces * LANES)
            size = here.stop - here.start
            tall = jnp.concatenate([left[here], left_marks[here]], axis=1)
            scores = lax.dot_general(tall, wide, (((1,), (1,)), ((), ())), preferred_element_type=F32)
            best = scores[:, :LANES]
            for lane in range(LANES, columns, LANES):
                best = jnp.maximum(best, scores[:, lane : lane + LANES])
            rowmax.append(jnp.max(best.reshape(size // LANES, LANES, LANES), axis=2))
            over = jnp.max(scores.reshape(size // 8, 8, columns), axis=0)
            colmax = over if colmax is None else jnp.maximum(colmax, over)
    return jnp.concatenate(rowmax, axis=0), jnp.max(colmax, axis=0).reshape(columns // LANES, LANES)


def pack(vec, docs, own1, own2, own):
    tokens = vec.shape[0] - docs.shape[0]
    head = own1.shape[0] - docs.shape[0]
    tags = docs[...].astype(F32).astype(BF16)
    own1[:head] = vec[:head]
    own1[head:] = tags
    own2[...] = vec[head:tokens]
    own[:tokens] = vec[:tokens]
    own[tokens:] = tags


def after(value, *others):
    return lax.optimization_barrier((value, *others))[0]


def per_device(slabs, count, vectors, docs, prior):
    axes = ("slab", "corpus")
    tokens, dim = vectors.shape
    lines = tokens // LANES
    head = tokens * HEAD // 16
    part = head // LANES
    rest = lines - part
    layer, ring, pair, beside = routes(slabs, count)
    block = lax.axis_index("corpus")
    block = jnp.where(lax.axis_index("slab") % 2 == 1, count - 1 - block, block)
    has_pair = (block % ROUNDS >= 2).astype(jnp.int32).reshape(1)
    far = jnp.where(block % ROUNDS == 0, block == count - ROUNDS, block < ROUNDS)
    far = (far & (lax.axis_index("corpus") < ROUNDS)).astype(jnp.int32).reshape(1)
    marks = struct(tokens, LANES, dtype=BF16)
    marks1, marks2 = struct(head, LANES, dtype=BF16), struct(tokens - head, LANES, dtype=BF16)
    smem = pl.BlockSpec(memory_space=pltpu.SMEM)
    vmem = pl.BlockSpec(memory_space=pltpu.VMEM)
    whole, piece1, piece2 = struct(lines, LANES), struct(part, LANES), struct(rest, LANES)

    own1, own2, own = call(
        "pack",
        pack,
        [jnp.pad(vectors, ((0, lines), (0, 0))), docs.reshape(lines, LANES)],
        [struct(rows, dim, dtype=BF16) for rows in (head + lines, tokens - head, tokens + lines)],
    )
    p1 = lax.ppermute(own1, axes, ring)
    z1 = lax.ppermute(own1, axes, layer)
    q = lax.ppermute(own, axes, pair)
    p2 = lax.ppermute(own2, axes, ring)
    z2 = lax.ppermute(own2, axes, layer)

    def own_marks(own, out):
        mark(own[tokens:], out, -MARK)

    (own_m,) = call("own_marks", own_marks, [own], [marks])

    def ring1(own, own_m, p1, p_m1, p_m2, own_out, p_out):
        mark(p1[head : head + part], p_m1, MARK)
        mark(p1[head + part :], p_m2, MARK)
        p_out[...], own_out[...] = tile([(p1[:head], p_m1[...])], [(own[:tokens], own_m[...])])

    p_m1, p_m2, own_max, p1_max = call("ring1", ring1, [own, own_m, p1], [marks1, marks2, whole, piece1])

    def layer1(own, own_m, p1, p_m1, z1, own_max, p_max, z_m1, z_m2, own_out, p_out, z_out):
        mark(z1[head : head + part], z_m1, MARK)
        mark(z1[head + part :], z_m2, MARK)
        row, col = tile([(z1[:head], z_m1[...])], [(own[:tokens], own_m[...]), (p1[:head], -p_m1[...])])
        own_out[...] = jnp.maximum(own_max[...], col[:lines])
        p_out[...] = jnp.maximum(p_max[...], col[lines:])
        z_out[...] = row

    z_m1, z_m2, own_max, p1_max, z1_max = call(
        "layer1",
        layer1,
        [own, own_m, p1, p_m1, z1, own_max, p1_max],
        [marks1, marks2, whole, piece1, piece1],
    )

    def second(p1, p_m1, p2, p_m2, z1, z_m1, z2, z_m2, z1_max, p1_max, z_out, p_out):
        row1, col1 = tile([(z2[...], -z_m2[...])], [(p1[:head], p_m1[...]), (p2[...], p_m2[...])])
        row2, col2 = tile([(p2[...], -p_m2[...])], [(z1[:head], z_m1[...])])
        z_out[:part] = jnp.maximum(z1_max[...], col2)
        z_out[part:] = row1
        p_out[:part] = jnp.maximum(p1_max[...], col1[:part])
        p_out[part:] = jnp.maximum(col1[part:], row2)

    z_max, p_max = call(
        "second", second, [p1, p_m1, p2, p_m2, z1, z_m1, z2, z_m2, z1_max, p1_max], [whole, whole]
    )
    r = lax.ppermute(after(q, z_max), axes, beside)

    def layer2(own, own_m, z2, z_m2, own_max, z_max, own_out, z_out):
        row, col = tile([(z2[...], z_m2[...])], [(own[:tokens], own_m[...])])
        own_out[...] = jnp.maximum(own_max[...], col)
        z_out[:part] = z_max[:part]
        z_out[part:] = jnp.maximum(z_max[part:], row)

    own_max, z_max = call("layer2", layer2, [own, own_m, z2, z_m2, own_max, z_max], [whole, whole])

    def q_marks(q, after, out):
        mark(q[tokens:], out, MARK)

    (q_m,) = call("q_marks", q_marks, [q, own_max], [marks])

    def pairs(has, z1, z2, q, q_m, r, z_max, z_out, out, other_m):
        z_out[lines:] = jnp.full((3 * lines, LANES), NEG, F32)

        @pl.when(has[0] > 0)
        def _():
            mark(z1[head:], other_m, -MARK)
            row, col = tile([(z1[:head], other_m[:head]), (z2[...], other_m[head:])], [(q[:tokens], q_m[...])])
            z_out[:lines] = jnp.maximum(z_max[...], row)
            out[:lines] = jnp.full((lines, LANES), NEG, F32)
            out[lines:] = col

        @pl.when(has[0] == 0)
        def _():
            mark(r[tokens:], other_m, -MARK)
            z_out[:lines] = z_max[...]
            out[:lines], out[lines:] = tile([(q[:tokens], q_m[...])], [(r[:tokens], other_m[...])])

    z_max, mine = call(
        "pairs",
        pairs,
        [has_pair, z1, z2, q, q_m, r, z_max],
        [struct(4 * lines, LANES), struct(2 * lines, LANES)],
        specs=[smem] + [vmem] * 6,
        scratch=[pltpu.VMEM((tokens, LANES), BF16)],
    )
    theirs = lax.ppermute(mine, axes, beside)

    def ring2(wanted, far, own, own_m, p2, p_m2, own_max, p_max, own_out, p_out):
        @pl.when(far[0] == wanted)
        def _():
            row, col = tile([(p2[...], p_m2[...])], [(own[:tokens], own_m[...])])
            own_out[...] = jnp.maximum(own_max[...], col)
            p_out[:part] = p_max[:part]
            p_out[part:] = jnp.maximum(p_max[part:], row)

        @pl.when(far[0] != wanted)
        def _():
            own_out[...] = own_max[...]
            p_out[...] = p_max[...]

    p_max = after(p_max, mine)
    for wanted in (1, 0):
        own_max, p_max = call(
            "ring2",
            functools.partial(ring2, wanted),
            [far, own, own_m, p2, p_m2, own_max, p_max],
            [whole, whole],
            specs=[smem] + [vmem] * 6,
        )
        if wanted:
            z_back = lax.ppermute(after(z_max, p_max), axes, backwards(layer))
    p_back = lax.ppermute(p_max, axes, backwards(ring))

    def merge(has, mine, theirs, own_max, own_out, q_out):
        got = jnp.where(has[0] > 0, theirs[...], F32(NEG))
        own_out[...] = jnp.maximum(own_max[...], got[:lines])
        q_out[...] = jnp.maximum(mine[lines:], got[lines:])

    own_max, q_max = call(
        "merge", merge, [has_pair, mine, theirs, own_max], [whole, whole], specs=[smem] + [vmem] * 3
    )
    q_back = lax.ppermute(q_max, axes, backwards(pair))
    q_back = jnp.where(has_pair > 0, NEG, q_back)
    best = jnp.maximum(jnp.maximum(own_max, z_back[:lines]), jnp.maximum(p_back, q_back))
    return jnp.maximum(prior, best.reshape(tokens))


def solution(mesh):
    spec = P(("slab", "corpus"))
    return jax.shard_map(
        functools.partial(per_device, mesh.shape["slab"], mesh.shape["corpus"]),
        mesh=mesh,
        in_specs=(spec, spec, spec),
        out_specs=spec,
        check_vma=False,
    )
```

```python
import functools

import jax
import jax.numpy as jnp
from jax import lax
from jax.experimental import pallas as pl
from jax.experimental.pallas import tpu as pltpu
from jax.sharding import PartitionSpec as P

ROUNDS = 4
NEG = -1e30
MARK = 2.0**50
LANES = 128
ROWS = 512
VMEM = 24 * 2**20
F32 = jnp.float32
BF16 = jnp.bfloat16
HEAD = 10


def routes(slabs, count):
    layer, ring, pair, beside = [], [], [], []
    for slab in range(slabs):
        for block in range(count):
            place = block % ROUNDS

            def device(position, slab=slab):
                position = position % count
                return slab * count + (count - 1 - position if slab % 2 else position)

            here, other = device(block), device(count - 1 - block, slab ^ 1)
            layer.append((here, device(block - ROUNDS if place == 0 else block + ROUNDS)))
            ring.append((here, device(block - place + (place + 1) % ROUNDS)))
            pair.append((here, device(block + 2) if place < 2 else other))
            beside.append((here, other))
    return layer, ring, pair, beside


def backwards(pairs):
    return [(target, source) for source, target in pairs]


def struct(*shape, dtype=F32):
    return jax.ShapeDtypeStruct(shape, dtype)


def call(name, kernel, operands, outs, specs=None, scratch=()):
    moved = sum(x.size * x.dtype.itemsize for x in list(operands) + list(outs))
    return pl.pallas_call(
        kernel,
        out_shape=outs,
        in_specs=specs or [pl.BlockSpec(memory_space=pltpu.VMEM)] * len(operands),
        out_specs=[pl.BlockSpec(memory_space=pltpu.VMEM)] * len(outs),
        scratch_shapes=scratch,
        compiler_params=pltpu.CompilerParams(vmem_limit_bytes=VMEM),
        cost_estimate=pl.CostEstimate(flops=0, bytes_accessed=moved, transcendentals=0),
        name=name,
    )(*operands)


def mark(tags, out, value, first=0):
    lane = lax.broadcasted_iota(jnp.int32, (LANES, LANES), 0).astype(F32)
    tags = tags.astype(F32)
    for row in range(out.shape[0] // LANES):
        hit = jnp.where(tags[first + row : first + row + 1] == lane, F32(value), F32(0.0))
        out[row * LANES : (row + 1) * LANES] = hit.T.astype(BF16)


def tile(lefts, rights):
    wide = jnp.concatenate([jnp.concatenate(pair, axis=1) for pair in rights], axis=0)
    columns = wide.shape[0]
    colmax, rowmax = None, []
    for left, left_marks in lefts:
        count = left.shape[0] // LANES
        pieces = -(-count * LANES // ROWS)
        for piece in range(pieces):
            here = slice(piece * count // pieces * LANES, (piece + 1) * count // pieces * LANES)
            size = here.stop - here.start
            tall = jnp.concatenate([left[here], left_marks[here]], axis=1)
            scores = lax.dot_general(tall, wide, (((1,), (1,)), ((), ())), preferred_element_type=F32)
            best = scores[:, :LANES]
            for lane in range(LANES, columns, LANES):
                best = jnp.maximum(best, scores[:, lane : lane + LANES])
            rowmax.append(jnp.max(best.reshape(size // LANES, LANES, LANES), axis=2))
            over = jnp.max(scores.reshape(size // 8, 8, columns), axis=0)
            colmax = over if colmax is None else jnp.maximum(colmax, over)
    return jnp.concatenate(rowmax, axis=0), jnp.max(colmax, axis=0).reshape(columns // LANES, LANES)


def pack(vec, docs, own1, own2, own):
    tokens = vec.shape[0] - docs.shape[0]
    head = own1.shape[0] - docs.shape[0]
    tags = docs[...].astype(F32).astype(BF16)
    own1[:head] = vec[:head]
    own1[head:] = tags
    own2[...] = vec[head:tokens]
    own[:tokens] = vec[:tokens]
    own[tokens:] = tags


def after(value, *others):
    return lax.optimization_barrier((value, *others))[0]


def per_device(slabs, count, vectors, docs, prior):
    axes = ("slab", "corpus")
    tokens, dim = vectors.shape
    lines = tokens // LANES
    head = tokens * HEAD // 16
    part = head // LANES
    rest = lines - part
    layer, ring, pair, beside = routes(slabs, count)
    block = lax.axis_index("corpus")
    block = jnp.where(lax.axis_index("slab") % 2 == 1, count - 1 - block, block)
    has_pair = (block % ROUNDS >= 2).astype(jnp.int32).reshape(1)
    far = jnp.where(block % ROUNDS == 0, block == count - ROUNDS, block < ROUNDS)
    far = (far & (lax.axis_index("corpus") < ROUNDS)).astype(jnp.int32).reshape(1)
    marks = struct(tokens, LANES, dtype=BF16)
    marks1, marks2 = struct(head, LANES, dtype=BF16), struct(tokens - head, LANES, dtype=BF16)
    smem = pl.BlockSpec(memory_space=pltpu.SMEM)
    vmem = pl.BlockSpec(memory_space=pltpu.VMEM)
    whole, piece1, piece2 = struct(lines, LANES), struct(part, LANES), struct(rest, LANES)

    own1, own2, own = call(
        "pack",
        pack,
        [jnp.pad(vectors, ((0, lines), (0, 0))), docs.reshape(lines, LANES)],
        [struct(rows, dim, dtype=BF16) for rows in (head + lines, tokens - head, tokens + lines)],
    )
    p1 = lax.ppermute(own1, axes, ring)
    z1 = lax.ppermute(own1, axes, layer)
    q = lax.ppermute(own, axes, pair)
    p2 = lax.ppermute(own2, axes, ring)
    z2 = lax.ppermute(own2, axes, layer)

    def own_marks(own, out):
        mark(own[tokens:], out, -MARK)

    (own_m,) = call("own_marks", own_marks, [own], [marks])

    def ring1(own, own_m, p1, p_m1, p_m2, own_out, p_out):
        mark(p1[head:], p_m1, MARK)
        mark(p1[head:], p_m2, MARK, part)
        p_out[...], own_out[...] = tile([(p1[:head], p_m1[...])], [(own[:tokens], own_m[...])])

    p_m1, p_m2, own_max, p1_max = call("ring1", ring1, [own, own_m, p1], [marks1, marks2, whole, piece1])

    def layer1(own, own_m, p1, p_m1, z1, own_max, p_max, z_m1, z_m2, own_out, p_out, z_out):
        mark(z1[head:], z_m1, MARK)
        mark(z1[head:], z_m2, MARK, part)
        row, col = tile([(z1[:head], z_m1[...])], [(own[:tokens], own_m[...]), (p1[:head], -p_m1[...])])
        own_out[...] = jnp.maximum(own_max[...], col[:lines])
        p_out[...] = jnp.maximum(p_max[...], col[lines:])
        z_out[...] = row

    z_m1, z_m2, own_max, p1_max, z1_max = call(
        "layer1",
        layer1,
        [own, own_m, p1, p_m1, z1, own_max, p1_max],
        [marks1, marks2, whole, piece1, piece1],
    )

    def second(p1, p_m1, p2, p_m2, z1, z_m1, z2, z_m2, z1_max, p1_max, z_out, p_out):
        row1, col1 = tile([(z2[...], -z_m2[...])], [(p1[:head], p_m1[...]), (p2[...], p_m2[...])])
        row2, col2 = tile([(p2[...], -p_m2[...])], [(z1[:head], z_m1[...])])
        z_out[:part] = jnp.maximum(z1_max[...], col2)
        z_out[part:] = row1
        p_out[:part] = jnp.maximum(p1_max[...], col1[:part])
        p_out[part:] = jnp.maximum(col1[part:], row2)

    z_max, p_max = call(
        "second", second, [p1, p_m1, p2, p_m2, z1, z_m1, z2, z_m2, z1_max, p1_max], [whole, whole]
    )
    r = lax.ppermute(after(q, z_max), axes, beside)

    def layer2(own, own_m, z2, z_m2, own_max, z_max, own_out, z_out):
        row, col = tile([(z2[...], z_m2[...])], [(own[:tokens], own_m[...])])
        own_out[...] = jnp.maximum(own_max[...], col)
        z_out[:part] = z_max[:part]
        z_out[part:] = jnp.maximum(z_max[part:], row)

    own_max, z_max = call("layer2", layer2, [own, own_m, z2, z_m2, own_max, z_max], [whole, whole])

    def q_marks(q, after, out):
        mark(q[tokens:], out, MARK)

    (q_m,) = call("q_marks", q_marks, [q, own_max], [marks])

    def pairs(has, z1, z2, q, q_m, r, z_max, z_out, out, other_m):
        z_out[lines:] = jnp.full((3 * lines, LANES), NEG, F32)

        @pl.when(has[0] > 0)
        def _():
            mark(z1[head:], other_m, -MARK)
            row, col = tile([(z1[:head], other_m[:head]), (z2[...], other_m[head:])], [(q[:tokens], q_m[...])])
            z_out[:lines] = jnp.maximum(z_max[...], row)
            out[:lines] = jnp.full((lines, LANES), NEG, F32)
            out[lines:] = col

        @pl.when(has[0] == 0)
        def _():
            mark(r[tokens:], other_m, -MARK)
            z_out[:lines] = z_max[...]
            out[:lines], out[lines:] = tile([(q[:tokens], q_m[...])], [(r[:tokens], other_m[...])])

    z_max, mine = call(
        "pairs",
        pairs,
        [has_pair, z1, z2, q, q_m, r, z_max],
        [struct(4 * lines, LANES), struct(2 * lines, LANES)],
        specs=[smem] + [vmem] * 6,
        scratch=[pltpu.VMEM((tokens, LANES), BF16)],
    )
    theirs = lax.ppermute(mine, axes, beside)

    def ring2(wanted, far, own, own_m, p2, p_m2, own_max, p_max, own_out, p_out):
        @pl.when(far[0] == wanted)
        def _():
            row, col = tile([(p2[...], p_m2[...])], [(own[:tokens], own_m[...])])
            own_out[...] = jnp.maximum(own_max[...], col)
            p_out[:part] = p_max[:part]
            p_out[part:] = jnp.maximum(p_max[part:], row)

        @pl.when(far[0] != wanted)
        def _():
            own_out[...] = own_max[...]
            p_out[...] = p_max[...]

    p_max = after(p_max, mine)
    for wanted in (1, 0):
        own_max, p_max = call(
            "ring2",
            functools.partial(ring2, wanted),
            [far, own, own_m, p2, p_m2, own_max, p_max],
            [whole, whole],
            specs=[smem] + [vmem] * 6,
        )
        if wanted:
            z_back = lax.ppermute(after(z_max, p_max), axes, backwards(layer))
    p_back = lax.ppermute(p_max, axes, backwards(ring))

    def merge(has, mine, theirs, own_max, own_out, q_out):
        got = jnp.where(has[0] > 0, theirs[...], F32(NEG))
        own_out[...] = jnp.maximum(own_max[...], got[:lines])
        q_out[...] = jnp.maximum(mine[lines:], got[lines:])

    own_max, q_max = call(
        "merge", merge, [has_pair, mine, theirs, own_max], [whole, whole], specs=[smem] + [vmem] * 3
    )
    q_back = lax.ppermute(q_max, axes, backwards(pair))
    q_back = jnp.where(has_pair > 0, NEG, q_back)
    best = jnp.maximum(jnp.maximum(own_max, z_back[:lines]), jnp.maximum(p_back, q_back))
    return jnp.maximum(prior, best.reshape(tokens))


def solution(mesh):
    spec = P(("slab", "corpus"))
    return jax.shard_map(
        functools.partial(per_device, mesh.shape["slab"], mesh.shape["corpus"]),
        mesh=mesh,
        in_specs=(spec, spec, spec),
        out_specs=spec,
        check_vma=False,
    )
```

```python
import functools

import jax
import jax.numpy as jnp
from jax import lax
from jax.experimental import pallas as pl
from jax.experimental.pallas import tpu as pltpu
from jax.sharding import PartitionSpec as P

ROUNDS = 4
NEG = -1e30
MARK = 2.0**50
LANES = 128
ROWS = 512
VMEM = 24 * 2**20
F32 = jnp.float32
BF16 = jnp.bfloat16
HEAD = 9


def routes(slabs, count):
    layer, ring, pair, beside, across = [], [], [], [], []
    for slab in range(slabs):
        for block in range(count):
            place = block % ROUNDS

            def device(position, slab=slab):
                position = position % count
                return slab * count + (count - 1 - position if slab % 2 else position)

            here, other = device(block), device(count - 1 - block, slab ^ 1)
            layer.append((here, device(block - ROUNDS if place == 0 else block + ROUNDS)))
            ring.append((here, device(block - place + (place + 1) % ROUNDS)))
            pair.append((here, device(block + 2) if place < 2 else other))
            beside.append((here, other))
            aim = count - 1 - block + (-2 if place < 2 else 2)
            across.append((here, device(aim, slab ^ 1)))
    return layer, ring, pair, beside, across


def backwards(pairs):
    return [(target, source) for source, target in pairs]


def struct(*shape, dtype=F32):
    return jax.ShapeDtypeStruct(shape, dtype)


def call(name, kernel, operands, outs, specs=None, scratch=()):
    moved = sum(x.size * x.dtype.itemsize for x in list(operands) + list(outs))
    return pl.pallas_call(
        kernel,
        out_shape=outs,
        in_specs=specs or [pl.BlockSpec(memory_space=pltpu.VMEM)] * len(operands),
        out_specs=[pl.BlockSpec(memory_space=pltpu.VMEM)] * len(outs),
        scratch_shapes=scratch,
        compiler_params=pltpu.CompilerParams(vmem_limit_bytes=VMEM),
        cost_estimate=pl.CostEstimate(flops=0, bytes_accessed=moved, transcendentals=0),
        name=name,
    )(*operands)


def mark(tags, out, value, first=0):
    lane = lax.broadcasted_iota(jnp.int32, (LANES, LANES), 0).astype(F32)
    tags = tags.astype(F32)
    for row in range(out.shape[0] // LANES):
        hit = jnp.where(tags[first + row : first + row + 1] == lane, F32(value), F32(0.0))
        out[row * LANES : (row + 1) * LANES] = hit.T.astype(BF16)


def tile(lefts, rights):
    wide = jnp.concatenate([jnp.concatenate(pair, axis=1) for pair in rights], axis=0)
    columns = wide.shape[0]
    colmax, rowmax = None, []
    for left, left_marks in lefts:
        count = left.shape[0] // LANES
        pieces = -(-count * LANES // ROWS)
        for piece in range(pieces):
            here = slice(piece * count // pieces * LANES, (piece + 1) * count // pieces * LANES)
            size = here.stop - here.start
            tall = jnp.concatenate([left[here], left_marks[here]], axis=1)
            scores = lax.dot_general(tall, wide, (((1,), (1,)), ((), ())), preferred_element_type=F32)
            best = scores[:, :LANES]
            for lane in range(LANES, columns, LANES):
                best = jnp.maximum(best, scores[:, lane : lane + LANES])
            rowmax.append(jnp.max(best.reshape(size // LANES, LANES, LANES), axis=2))
            over = jnp.max(scores.reshape(size // 8, 8, columns), axis=0)
            colmax = over if colmax is None else jnp.maximum(colmax, over)
    return jnp.concatenate(rowmax, axis=0), jnp.max(colmax, axis=0).reshape(columns // LANES, LANES)


def pack(vec, docs, own1, own2, own):
    tokens = vec.shape[0] - docs.shape[0]
    head = own1.shape[0] - docs.shape[0]
    tags = docs[...].astype(F32).astype(BF16)
    own1[:head] = vec[:head]
    own1[head:] = tags
    own2[...] = vec[head:tokens]
    own[:tokens] = vec[:tokens]
    own[tokens:] = tags


def after(value, *others):
    return lax.optimization_barrier((value, *others))[0]


def per_device(slabs, count, vectors, docs, prior):
    axes = ("slab", "corpus")
    tokens, dim = vectors.shape
    lines = tokens // LANES
    head = tokens * HEAD // 16
    part = head // LANES
    rest = lines - part
    layer, ring, pair, beside, across = routes(slabs, count)
    block = lax.axis_index("corpus")
    block = jnp.where(lax.axis_index("slab") % 2 == 1, count - 1 - block, block)
    has_pair = (block % ROUNDS >= 2).astype(jnp.int32).reshape(1)
    far = jnp.where(block % ROUNDS == 0, block == count - ROUNDS, block < ROUNDS)
    far = (far & (lax.axis_index("corpus") < ROUNDS)).astype(jnp.int32).reshape(1)
    marks = struct(tokens, LANES, dtype=BF16)
    marks1, marks2 = struct(head, LANES, dtype=BF16), struct(tokens - head, LANES, dtype=BF16)
    smem = pl.BlockSpec(memory_space=pltpu.SMEM)
    vmem = pl.BlockSpec(memory_space=pltpu.VMEM)
    whole, piece1, piece2 = struct(lines, LANES), struct(part, LANES), struct(rest, LANES)

    own1, own2, own = call(
        "pack",
        pack,
        [jnp.pad(vectors, ((0, lines), (0, 0))), docs.reshape(lines, LANES)],
        [struct(rows, dim, dtype=BF16) for rows in (head + lines, tokens - head, tokens + lines)],
    )
    p1 = lax.ppermute(own1, axes, ring)
    z1 = lax.ppermute(own1, axes, layer)
    q = lax.ppermute(own, axes, pair)
    p2 = lax.ppermute(own2, axes, ring)
    z2 = lax.ppermute(own2, axes, layer)

    def own_marks(own, out):
        mark(own[tokens:], out, -MARK)

    (own_m,) = call("own_marks", own_marks, [own], [marks])

    def ring1(own, own_m, p1, p_m1, p_m2, own_out, p_out):
        mark(p1[head:], p_m1, MARK)
        mark(p1[head:], p_m2, MARK, part)
        p_out[...], own_out[...] = tile([(p1[:head], p_m1[...])], [(own[:tokens], own_m[...])])

    p_m1, p_m2, own_max, p1_max = call("ring1", ring1, [own, own_m, p1], [marks1, marks2, whole, piece1])

    def layer1(own, own_m, p1, p_m1, z1, own_max, p_max, z_m1, z_m2, own_out, p_out, z_out):
        mark(z1[head:], z_m1, MARK)
        mark(z1[head:], z_m2, MARK, part)
        row, col = tile([(z1[:head], z_m1[...])], [(own[:tokens], own_m[...]), (p1[:head], -p_m1[...])])
        own_out[...] = jnp.maximum(own_max[...], col[:lines])
        p_out[...] = jnp.maximum(p_max[...], col[lines:])
        z_out[...] = row

    z_m1, z_m2, own_max, p1_max, z1_max = call(
        "layer1",
        layer1,
        [own, own_m, p1, p_m1, z1, own_max, p1_max],
        [marks1, marks2, whole, piece1, piece1],
    )

    def second(p1, p_m1, p2, p_m2, z1, z_m1, z2, z_m2, z1_max, p1_max, z_out, p_out):
        row1, col1 = tile([(z2[...], -z_m2[...])], [(p1[:head], p_m1[...]), (p2[...], p_m2[...])])
        row2, col2 = tile([(p2[...], -p_m2[...])], [(z1[:head], z_m1[...])])
        z_out[:part] = jnp.maximum(z1_max[...], col2)
        z_out[part:] = row1
        p_out[:part] = jnp.maximum(p1_max[...], col1[:part])
        p_out[part:] = jnp.maximum(col1[part:], row2)

    z_max, p_max = call(
        "second", second, [p1, p_m1, p2, p_m2, z1, z_m1, z2, z_m2, z1_max, p1_max], [whole, whole]
    )
    r = lax.ppermute(after(q, z_max), axes, beside)

    def inner(has, own, own_m, z1, z2, z_m2, p2, p_m2, q, own_max, z_max, p_max, own_out, z_out, p_out, out,
              q_m, z_m):
        z_out[lines:] = jnp.full((7 * lines, LANES), NEG, F32)
        row, col = tile([(z2[...], z_m2[...])], [(own[:tokens], own_m[...])])
        p_out[:part] = p_max[:part]
        p_out[lines:] = jnp.full((3 * lines, LANES), NEG, F32)

        @pl.when(has[0] > 0)
        def _():
            mark(q[tokens:], q_m, MARK)
            mark(z1[head:], z_m, -MARK)
            z_row, q_col = tile([(z1[:head], z_m[:head]), (z2[...], z_m[head:])], [(q[:tokens], q_m[...])])
            z_out[:part] = jnp.maximum(z_max[:part], z_row[:part])
            z_out[part:lines] = jnp.maximum(jnp.maximum(z_max[part:], row), z_row[part:])
            own_out[...] = jnp.maximum(own_max[...], col)
            p_out[part:lines] = p_max[part:]
            out[:lines] = jnp.full((lines, LANES), NEG, F32)
            out[lines:] = q_col

        @pl.when(has[0] == 0)
        def _():
            p_row, p_col = tile([(p2[...], p_m2[...])], [(own[:tokens], own_m[...])])
            z_out[:part] = z_max[:part]
            z_out[part:lines] = jnp.maximum(z_max[part:], row)
            own_out[...] = jnp.maximum(jnp.maximum(own_max[...], col), p_col)
            p_out[part:lines] = jnp.maximum(p_max[part:], p_row)
            out[...] = jnp.full((2 * lines, LANES), NEG, F32)

    own_max, z_max, p_max, mine = call(
        "inner",
        inner,
        [has_pair, own, own_m, z1, z2, z_m2, p2, p_m2, q, own_max, z_max, p_max],
        [whole, struct(8 * lines, LANES), struct(4 * lines, LANES), struct(2 * lines, LANES)],
        specs=[smem] + [vmem] * 11,
        scratch=[pltpu.VMEM((tokens, LANES), BF16)] * 2,
    )

    def outer(wanted, far, has, own, own_m, p2, p_m2, q, r, own_max, p_max, mine, own_out, p_out, out, q_m, r_m):
        own_out[...] = own_max[...]
        p_out[...] = p_max[...]
        out[...] = mine[...]

        @pl.when((far[0] == wanted) & (has[0] > 0))
        def _():
            row, col = tile([(p2[...], p_m2[...])], [(own[:tokens], own_m[...])])
            own_out[...] = jnp.maximum(own_max[...], col)
            p_out[part:lines] = jnp.maximum(p_max[part:lines], row)

        @pl.when((far[0] == wanted) & (has[0] == 0))
        def _():
            mark(q[tokens:], q_m, MARK)
            mark(r[tokens:], r_m, -MARK)
            out[:lines], out[lines:] = tile([(q[:tokens], q_m[...])], [(r[:tokens], r_m[...])])

    for wanted in (1, 0):
        own_max, p_max, mine = call(
            "outer",
            functools.partial(outer, wanted),
            [far, has_pair, own, own_m, p2, p_m2, q, r, own_max, p_max, mine],
            [whole, struct(4 * lines, LANES), struct(2 * lines, LANES)],
            specs=[smem] * 2 + [vmem] * 9,
            scratch=[pltpu.VMEM((tokens, LANES), BF16)] * 2,
        )
        if wanted:
            z_back = lax.ppermute(after(z_max, own_max), axes, backwards(layer))
    q_back = lax.ppermute(mine, axes, backwards(pair))
    r_back = lax.ppermute(mine, axes, across)
    p_back = lax.ppermute(p_max, axes, backwards(ring))
    pair_back = jnp.where(has_pair > 0, q_back[:lines], jnp.maximum(q_back[lines:], r_back[lines:]))
    best = jnp.maximum(jnp.maximum(own_max, z_back[:lines]), jnp.maximum(p_back[:lines], pair_back))
    return jnp.maximum(prior, best.reshape(tokens))


def solution(mesh):
    spec = P(("slab", "corpus"))
    return jax.shard_map(
        functools.partial(per_device, mesh.shape["slab"], mesh.shape["corpus"]),
        mesh=mesh,
        in_specs=(spec, spec, spec),
        out_specs=spec,
        check_vma=False,
    )
```
